32 devices in a mesh: dp: 16 (over z, y, core), seq: 2 (over x).
Axes of the slice: x: 2, y: 2, z: 4, core: 2. Of those that a mesh axis runs over, the one named last changes fastest.
Arguments:
- query_rows: bfloat16 [16, 1536, 2048], P('dp', 'seq'), may hold values from -6 to 6
- key_rows: bfloat16 [16, 1536, 2048], P('dp', 'seq'), may hold values from -6 to 6
- value_rows: bfloat16 [16, 1536, 2048], P('dp', 'seq'), may hold values from -6 to 6
- key_tiles: int32 [16, 4, 4], replicated, may hold values from 0 to 3, as said below
- tile_counts: int32 [16, 4], replicated, may hold values from 1 to 4
- out_weight: bfloat16 [2048, 3072], P('dp'), may hold values from -1.25 to 1.25
- gate_scale: bfloat16 [16, 3072], P('dp'), may hold values from 0.5 to 1.5
- residual: bfloat16 [16, 1536, 3072], P('dp', 'seq'), may hold values from -6 to 6
Outputs:
- block_out: bfloat16 [16, 1536, 3072], P('dp', 'seq')
The draws below stay inside these ranges and needn't reach their ends.
Inputs may be any that keep to these rules, and one draw needn't show every extreme that they name: Tiles form a grid of 2 frame positions by 2 height positions by 1 width positions; the tile at frame index a, height index b and width index c has the number a * 2 + b + c. The first tile_counts[h, s] entries of key_tiles[h, s, :] are, in increasing order, the distinct tiles of a box of this grid that contains tile s; the remaining entries equal s.
All inputs are finite; a program needn't handle non-finite values.
Results may differ from the reference program's by a relative error of at most 0.012.
Values may be sent and summed in bfloat16 or wider, within the bound.
No kernel may reach another device: no remote copies, remote signals or barrier semaphores. Data moves between devices by JAX's collectives and lax.ppermute only.
A program may use at most 128 MiB of HBM per device.

```python
import math
import jax
import jax.numpy as jnp
from jax import lax

D = 3072
HD = 128
HEADS = 16
TILE = 384
GT = 2
GH = 2
GW = 1
NTILES = 4
SEQLEN = 1536
CLIPS = 16


def draw_query_rows(key, part):
    key = jax.random.fold_in(key, 11)
    drawn = jnp.clip(jax.random.normal(key, (CLIPS, SEQLEN, HEADS, HD)), -4.0, 4.0)
    return drawn.reshape(CLIPS, SEQLEN, HEADS * HD).astype(jnp.bfloat16)


def draw_key_rows(key, part):
    key = jax.random.fold_in(key, 12)
    drawn = jnp.clip(jax.random.normal(key, (CLIPS, SEQLEN, HEADS, HD)), -4.0, 4.0)
    return drawn.reshape(CLIPS, SEQLEN, HEADS * HD).astype(jnp.bfloat16)


def window_pattern(key):
    key = jax.random.fold_in(key, 707)
    lottery = jax.random.randint(jax.random.fold_in(key, 1), (HEADS, 3), 0, 10)
    grid_dims = jnp.array([GT, GH, GW], jnp.int32)
    radius = jnp.where(lottery < 6, 0, jnp.where(lottery < 8, 1, grid_dims[None, :] - 1))
    ranking = jax.random.permutation(jax.random.fold_in(key, 2), HEADS)
    radius = jnp.where((ranking == 0)[:, None], grid_dims[None, :] - 1, radius)
    radius = jnp.where((ranking == 1)[:, None], 0, radius)
    radius = jnp.minimum(radius, grid_dims[None, :] - 1)
    tile_ids = jnp.arange(NTILES, dtype=jnp.int32)
    coords = jnp.stack([tile_ids // (GH * GW), tile_ids // GW % GH, tile_ids % GW], axis=1)
    low_end = jnp.maximum(coords[None, :, :] - radius[:, None, :], 0)
    high_end = jnp.minimum(coords[None, :, :] + radius[:, None, :], grid_dims[None, None, :] - 1)
    extent = high_end - low_end + 1
    counted = extent[:, :, 0] * extent[:, :, 1] * extent[:, :, 2]
    slot_ids = jnp.arange(NTILES, dtype=jnp.int32)[None, None, :]
    step_frames = slot_ids // (extent[:, :, 1:2] * extent[:, :, 2:3])
    step_height = slot_ids // extent[:, :, 2:3] % extent[:, :, 1:2]
    step_width = slot_ids % extent[:, :, 2:3]
    listed = ((low_end[:, :, 0:1] + step_frames) * GH + low_end[:, :, 1:2] + step_height) * GW + low_end[:, :, 2:3] + step_width
    listed = jnp.where(slot_ids < counted[:, :, None], listed, tile_ids[None, :, None])
    return (listed.astype(jnp.int32), counted.astype(jnp.int32))


def draw_key_tiles(key, part):
    return window_pattern(key)[0]


def draw_tile_counts(key, part):
    return window_pattern(key)[1]


def steps_of(rng, shape, cuts, smallest, high):
    def one(axis_at, parts):
        heights = jax.random.uniform(jax.random.fold_in(jax.random.fold_in(rng, 6), axis_at), (parts,), jnp.float32, smallest / len(cuts), high / len(cuts))
        return jnp.repeat(jnp.exp(heights), shape[axis_at] // parts).reshape((-1,) + (1,) * (len(shape) - axis_at - 1))

    factor_of = one(*cuts[0])
    for cut in cuts[1:]:
        factor_of = factor_of * one(*cut)
    return factor_of


def gaussian(stream_key, shape, spread, bound, shards=(), held_as=jnp.bfloat16):
    result = spread * jax.random.normal(stream_key, shape, jnp.float32)
    if shards:
        result = result * steps_of(stream_key, shape, shards, -0.22, 0.18)
    return jnp.clip(result, -bound, bound).astype(held_as)


def setup_inputs(seed: int = 0) -> dict:
    arg_keys = jax.random.split(jax.random.key(seed), 9)
    query_rows = draw_query_rows(jax.random.fold_in(arg_keys[8], 71), 0)
    key_rows = draw_key_rows(jax.random.fold_in(arg_keys[8], 71), 0)
    value_rows = gaussian(arg_keys[2], (CLIPS, SEQLEN, HEADS * HD), 1.0, 6.0, ((0, 16), (1, 2)))
    key_tiles = draw_key_tiles(jax.random.fold_in(arg_keys[8], 71), 0)
    tile_counts = draw_tile_counts(jax.random.fold_in(arg_keys[8], 71), 0)
    out_weight = gaussian(arg_keys[5], (HEADS * HD, D), (HEADS * HD * 4 // TILE) ** -0.5, 1.25, ((0, 16),))
    gate_scale = jnp.clip(0.5 + 1.0 * jax.random.uniform(arg_keys[6], (CLIPS, D), jnp.float32) ** steps_of(arg_keys[6], (CLIPS, D), ((0, 16),), -0.2, 0.2), 0.5, 1.5).astype(jnp.bfloat16)
    residual = gaussian(arg_keys[7], (CLIPS, SEQLEN, D), 1.0, 6.0, ((0, 16), (1, 2)))
    return dict(query_rows=query_rows, key_rows=key_rows, value_rows=value_rows, key_tiles=key_tiles, tile_counts=tile_counts, out_weight=out_weight, gate_scale=gate_scale, residual=residual)


def head_attention(query_head, key_head, value_head, visible):
    allowed = jnp.repeat(jnp.repeat(visible, TILE, axis=0), TILE, axis=1)
    scores = jnp.dot(query_head, key_head.T, preferred_element_type=jnp.float32) * (1.0 / math.sqrt(HD))
    row_peak = lax.optimization_barrier(jnp.max(jnp.where(allowed, scores, -jnp.inf), axis=1, keepdims=True))
    shifted = jnp.where(allowed, jnp.exp(scores - row_peak), 0.0)
    row_total = lax.optimization_barrier(jnp.sum(shifted, axis=1, keepdims=True))
    mixed = jnp.dot(shifted.astype(jnp.bfloat16), value_head, preferred_element_type=jnp.float32) / row_total
    return mixed.astype(jnp.bfloat16)

def reference(query_rows, key_rows, value_rows, key_tiles, tile_counts, out_weight, gate_scale, residual):
    slot_ids = jnp.arange(NTILES, dtype=jnp.int32)
    listed = (key_tiles[:, :, :, None] == slot_ids[None, None, None, :]) & (slot_ids[None, None, :, None] < tile_counts[:, :, None, None])
    visible = jnp.any(listed, axis=2)

    def one_clip(inputs):
        query_clip, key_clip, value_clip, gate_clip, residual_clip = inputs

        def one_head(head_index):
            first_col = (head_index * HD).astype(jnp.int32)
            query_head = lax.dynamic_slice_in_dim(query_clip, first_col, HD, 1)
            key_head = lax.dynamic_slice_in_dim(key_clip, first_col, HD, 1)
            value_head = lax.dynamic_slice_in_dim(value_clip, first_col, HD, 1)
            head_mask = lax.dynamic_index_in_dim(visible, head_index, 0, keepdims=False)
            return head_attention(query_head, key_head, value_head, head_mask)
        per_head = lax.map(one_head, jnp.arange(HEADS, dtype=jnp.int32))
        attended = jnp.transpose(per_head, (1, 0, 2)).reshape(SEQLEN, HEADS * HD)
        projected = jnp.dot(attended, out_weight, preferred_element_type=jnp.float32)
        mixed_out = residual_clip.astype(jnp.float32) + gate_clip.astype(jnp.float32)[None, :] * projected
        return mixed_out.astype(jnp.bfloat16)
    return lax.map(one_clip, (query_rows, key_rows, value_rows, gate_scale, residual))
```

```python
import functools
import math

import jax
import jax.numpy as jnp
from jax import lax
from jax.experimental import pallas as pl
from jax.experimental.pallas import tpu as pltpu
from jax.sharding import PartitionSpec as P

VMEM_LIMIT = 48 * 1024 * 1024


def slot_scores(query_blocks, key_blocks, value_blocks, head_tiles, slot_index, scale):
    chosen = lax.dynamic_index_in_dim(head_tiles, slot_index, 1, keepdims=False)
    near_keys = jnp.take(key_blocks, chosen, axis=0)
    near_values = jnp.take(value_blocks, chosen, axis=0)
    scores = (
        jnp.einsum("tqd,tkd->tqk", query_blocks, near_keys, preferred_element_type=jnp.float32)
        * scale
    )
    return (scores, near_values)


def attend_head(query_blocks, key_blocks, value_blocks, head_tiles, head_counts, scale):
    scores, near_values = slot_scores(query_blocks, key_blocks, value_blocks, head_tiles, 0, scale)
    row_peak = jnp.max(scores, axis=2)
    weights = jnp.exp(scores - row_peak[:, :, None])
    row_total = jnp.sum(weights, axis=2)
    running = jnp.einsum(
        "tqk,tkd->tqd",
        weights.astype(jnp.bfloat16),
        near_values,
        preferred_element_type=jnp.float32,
    )

    def one_slot(slot_index, carry):
        row_peak, row_total, running = carry
        scores, near_values = slot_scores(
            query_blocks, key_blocks, value_blocks, head_tiles, slot_index, scale
        )
        active = (slot_index < head_counts)[:, None]
        new_peak = jnp.where(active, jnp.maximum(row_peak, jnp.max(scores, axis=2)), row_peak)
        weights = jnp.where(active[:, :, None], jnp.exp(scores - new_peak[:, :, None]), 0.0)
        rescale = jnp.exp(row_peak - new_peak)
        row_total = row_total * rescale + jnp.sum(weights, axis=2)
        running = running * rescale[:, :, None] + jnp.einsum(
            "tqk,tkd->tqd",
            weights.astype(jnp.bfloat16),
            near_values,
            preferred_element_type=jnp.float32,
        )
        return (new_peak, row_total, running)

    last_slot = jnp.max(head_counts)
    row_peak, row_total, running = lax.fori_loop(
        1, last_slot, one_slot, (row_peak, row_total, running)
    )
    return (running / row_total[:, :, None]).astype(jnp.bfloat16)


def head_blocks(rows, first_col, head_dim, ntiles, tile_len):
    return rows[:, first_col : first_col + head_dim].reshape(ntiles, tile_len, head_dim)


def on_device_general(
    query_rows, key_rows, value_rows, key_tiles, tile_counts, out_weight, gate_scale, residual
):
    groups = lax.axis_size("seq")
    seq_index = lax.axis_index("seq")
    tok_rows = query_rows.shape[1]
    feat_width = query_rows.shape[2]
    head_count = key_tiles.shape[0]
    ntiles = key_tiles.shape[1]
    head_dim = feat_width // head_count
    local_heads = head_count // groups
    seqlen = tok_rows * groups
    tile_len = seqlen // ntiles
    scale = 1.0 / math.sqrt(head_dim)
    heads_query, heads_key, heads_value = (
        lax.all_to_all(rows[0], "seq", split_axis=1, concat_axis=0, tiled=True)
        for rows in (query_rows, key_rows, value_rows)
    )
    outputs = []
    for slot_head in range(local_heads):
        global_head = seq_index * local_heads + slot_head
        head_tiles = lax.dynamic_index_in_dim(key_tiles, global_head, 0, keepdims=False)
        head_counts = lax.dynamic_index_in_dim(tile_counts, global_head, 0, keepdims=False)
        first_col = slot_head * head_dim
        mixed_head = attend_head(
            head_blocks(heads_query, first_col, head_dim, ntiles, tile_len),
            head_blocks(heads_key, first_col, head_dim, ntiles, tile_len),
            head_blocks(heads_value, first_col, head_dim, ntiles, tile_len),
            head_tiles,
            head_counts,
            scale,
        )
        outputs.append(mixed_head.reshape(seqlen, head_dim))
    attended = jnp.concatenate(outputs, axis=1)
    token_major = lax.all_to_all(attended, "seq", split_axis=0, concat_axis=1, tiled=True)
    projected = jnp.dot(
        token_major,
        lax.all_gather(out_weight, "dp", axis=0, tiled=True),
        preferred_element_type=jnp.float32,
    )
    block_out = (
        residual[0].astype(jnp.float32) + gate_scale[0].astype(jnp.float32)[None, :] * projected
    )
    return block_out.astype(jnp.bfloat16)[None]


def plan_kernel(heads, ntiles, tiles_ref, counts_ref, order_ref, bits_ref, cross_ref):
    half = ntiles // 2

    def one_head(h, crossing):
        reach = jnp.int32(0)
        for s in range(ntiles):
            count = counts_ref[s, h]
            mask = jnp.int32(0)
            for slot in range(ntiles):
                bit = jnp.left_shift(jnp.int32(1), tiles_ref[s, slot, h])
                mask = mask | jnp.where(slot < count, bit, 0)
            bits_ref[h * ntiles + s] = mask
            other = ((1 << ntiles) - (1 << half)) if s < half else ((1 << half) - 1)
            reach = reach | (mask & other)
        is_cross = (reach != 0).astype(jnp.int32)
        place = jnp.where(is_cross == 1, crossing, heads - 1 - (h - crossing))
        order_ref[place] = h
        return crossing + is_cross

    cross_ref[0] = lax.fori_loop(0, heads, one_head, jnp.int32(0))


def make_plan(key_tiles, tile_counts):
    heads, ntiles, _ = key_tiles.shape
    smem = pl.BlockSpec(memory_space=pltpu.SMEM)
    return pl.pallas_call(
        functools.partial(plan_kernel, heads, ntiles),
        out_shape=(
            jax.ShapeDtypeStruct((heads,), jnp.int32),
            jax.ShapeDtypeStruct((heads * ntiles,), jnp.int32),
            jax.ShapeDtypeStruct((1,), jnp.int32),
        ),
        in_specs=[smem, smem],
        out_specs=(smem, smem, smem),
        name="plan",
    )(key_tiles.transpose(1, 2, 0), tile_counts.transpose(1, 0))


def pack_kernel(many, hd, order_ref, first_ref, key_ref, value_ref, out_ref, held, in_sems, out_sems):
    arriving, leaving = [], []
    for i in range(many):
        col = pl.multiple_of(order_ref[first_ref[0] + i] * hd, hd)
        for j, ref in enumerate((key_ref, value_ref)):
            k = 2 * i + j
            arriving.append(
                pltpu.make_async_copy(ref.at[:, pl.ds(col, hd)], held.at[i, j], in_sems.at[k])
            )
            leaving.append(pltpu.make_async_copy(held.at[i, j], out_ref.at[i, j], out_sems.at[k]))
    for copy in arriving:
        copy.start()
    for copy, onward in zip(arriving, leaving):
        copy.wait()
        onward.start()
    for onward in leaving:
        onward.wait()


def pack_heads(order, first, keys, values, many, hd):
    rows = keys.shape[0]
    smem = pl.BlockSpec(memory_space=pltpu.SMEM)
    anywhere = pl.BlockSpec(memory_space=pl.ANY)
    return pl.pallas_call(
        functools.partial(pack_kernel, many, hd),
        out_shape=jax.ShapeDtypeStruct((many, 2, rows, hd), keys.dtype),
        in_specs=[smem, smem, anywhere, anywhere],
        out_specs=anywhere,
        scratch_shapes=[
            pltpu.VMEM((many, 2, rows, hd), keys.dtype),
            pltpu.SemaphoreType.DMA((2 * many,)),
            pltpu.SemaphoreType.DMA((2 * many,)),
        ],
        compiler_params=pltpu.CompilerParams(vmem_limit_bytes=VMEM_LIMIT),
        cost_estimate=pl.CostEstimate(
            flops=0, bytes_accessed=many * 4 * rows * hd * 2, transcendentals=0
        ),
        name="pack",
    )(order, first.reshape(1), keys, values)


def attend(query, keys, values, exponent_scale):
    scores = [
        lax.dot_general(query, k, (((1,), (1,)), ((), ())), preferred_element_type=jnp.float32)
        for k in keys
    ]
    peak = functools.reduce(jnp.maximum, [jnp.max(s, axis=1, keepdims=True) for s in scores])
    weights = [jnp.exp2((s - peak) * exponent_scale) for s in scores]
    total = functools.reduce(jnp.add, [jnp.sum(w, axis=1, keepdims=True) for w in weights])
    mixed = functools.reduce(
        jnp.add,
        [
            jnp.dot(w.astype(jnp.bfloat16), v, preferred_element_type=jnp.float32)
            for w, v in zip(weights, values)
        ],
    )
    return (mixed * (1.0 / total)).astype(jnp.bfloat16)


def attention_kernel(
    heads, ntiles, tile_len, sub, scale, order_ref, bits_ref, place_ref, query, keys, values, far,
    _, out
):
    half = ntiles // 2
    rows = half * tile_len
    hd = query.shape[1] // heads
    start, crossing, seq_index, many, chunk_first = (place_ref[k] for k in range(5))
    near = heads - crossing
    near_first = seq_index * half
    far_first = half - near_first
    exponent_scale = scale * math.log2(math.e)

    def item_head(i):
        item = start + i
        return order_ref[jnp.where(item < near, crossing + item, item - near)]

    def column(i):
        return (0, item_head(i))

    def far_block(i):
        return (jnp.maximum(start + i - near - chunk_first, 0), 0, 0, 0)

    def one_item(q_ref, k_ref, v_ref, far_ref, out_ref):
        head = item_head(pl.program_id(0))

        def one_tile(tile, _):
            mask = bits_ref[head * ntiles + near_first + tile]
            wide = (lax.shift_right_logical(mask, near_first) & 3) == 3
            reach = (lax.shift_right_logical(mask, far_first) & 3) != 0
            base = pl.multiple_of(tile * tile_len, tile_len)
            own = pl.ds(base, tile_len)
            both = pl.ds(0, rows)

            def run(seen, use_far):
                near_keys = [k_ref[seen, :]]
                near_values = [v_ref[seen, :]]
                if use_far:
                    near_keys.append(far_ref[0, 0, seen, :])
                    near_values.append(far_ref[0, 1, seen, :])
                for part in range(tile_len // sub):
                    here = pl.ds(base + part * sub, sub)
                    out_ref[here, :] = attend(
                        q_ref[here, :], near_keys, near_values, exponent_scale
                    )

            narrow, inside = jnp.logical_not(wide), jnp.logical_not(reach)
            pl.when(wide & reach)(functools.partial(run, both, True))
            pl.when(narrow & reach)(functools.partial(run, own, True))
            pl.when(wide & inside)(functools.partial(run, both, False))
            pl.when(narrow & inside)(functools.partial(run, own, False))
            return 0

        lax.fori_loop(0, half, one_tile, 0)

    block = pl.BlockSpec((rows, hd), column)
    pipeline = pltpu.emit_pipeline(
        one_item,
        grid=(many,),
        in_specs=[block, block, block, pl.BlockSpec((1, 2, rows, hd), far_block)],
        out_specs=[block],
    )
    pl.when(many > 0)(lambda: pipeline(query, keys, values, far, out))


def attend_items(order, bits, place, qkv, far, attended, ntiles, hd, likely):
    query, keys, values = qkv
    rows, width = query.shape
    heads = width // hd
    tile_len = rows * 2 // ntiles
    smem = pl.BlockSpec(memory_space=pltpu.SMEM)
    anywhere = pl.BlockSpec(memory_space=pl.ANY)
    return pl.pallas_call(
        functools.partial(
            attention_kernel, heads, ntiles, tile_len, tile_len // 2, 1.0 / math.sqrt(hd)
        ),
        out_shape=jax.ShapeDtypeStruct((rows, width), query.dtype),
        in_specs=[smem] * 3 + [anywhere] * 5,
        out_specs=anywhere,
        input_output_aliases={7: 0},
        compiler_params=pltpu.CompilerParams(vmem_limit_bytes=VMEM_LIMIT),
        cost_estimate=pl.CostEstimate(
            flops=likely * 16 * rows * rows * hd,
            bytes_accessed=likely * rows * hd * 12,
            transcendentals=likely * 2 * rows * rows,
        ),
        name="attend",
    )(order, bits, place, query, keys, values, far, attended)


def empty_kernel(out_ref):
    pass


def unset(shape, dtype):
    return pl.pallas_call(
        empty_kernel,
        out_shape=jax.ShapeDtypeStruct(shape, dtype),
        out_specs=pl.BlockSpec(memory_space=pl.ANY),
        name="unset",
    )()


def project_kernel(sub, depth, split, rows_ref, att_ref, gate_ref, res_ref, *refs):
    shards, out_ref, weight = refs[:-2], refs[-2], refs[-1]
    block = pl.program_id(0)
    slot = 0

    def put(slot, ref):
        first = pl.multiple_of(rows_ref[slot] * depth, depth)
        weight[pl.ds(first, depth), :] = ref[...]

    per_core = len(shards) // 2
    for core in range(2):
        whole = shards[core * per_core : (core + 1) * per_core - 2]
        left, right = shards[(core + 1) * per_core - 2 : (core + 1) * per_core]
        for ref in whole:
            put(slot, ref)
            slot += 1
        pl.when(block < split)(functools.partial(put, slot, left))
        pl.when(block >= split)(functools.partial(put, slot, right))
        slot += 1

    gate = gate_ref[...].astype(jnp.float32)
    for part in range(att_ref.shape[0] // sub):
        here = pl.ds(part * sub, sub)
        projected = jnp.dot(att_ref[here, :], weight[...], preferred_element_type=jnp.float32)
        out_ref[here, :] = (res_ref[here, :].astype(jnp.float32) + gate * projected).astype(
            out_ref.dtype
        )


def project(attended, shard_rows, shards, gate, residual):
    rows, feats = attended.shape
    width = residual.shape[1]
    depth = shards[0].shape[0]
    block = 512
    split = width // 2 // block
    here = pl.BlockSpec((rows, block), lambda j, table: (0, j))
    whole = pl.BlockSpec((depth, block), lambda j, table: (0, j))
    left = pl.BlockSpec((depth, block), lambda j, table: (0, jnp.minimum(j, split - 1)))
    right = pl.BlockSpec((depth, block), lambda j, table: (0, jnp.maximum(j - split, 0)))
    per_core = len(shards) // 2
    return pl.pallas_call(
        functools.partial(project_kernel, 256, depth, split),
        out_shape=jax.ShapeDtypeStruct(residual.shape, residual.dtype),
        grid_spec=pltpu.PrefetchScalarGridSpec(
            num_scalar_prefetch=1,
            grid=(width // block,),
            in_specs=[
                pl.BlockSpec((rows, feats), lambda j, table: (0, 0)),
                pl.BlockSpec((1, block), lambda j, table: (0, j)),
                here,
            ]
            + ([whole] * (per_core - 2) + [left, right]) * 2,
            out_specs=here,
            scratch_shapes=[pltpu.VMEM((feats, block), attended.dtype)],
        ),
        compiler_params=pltpu.CompilerParams(vmem_limit_bytes=VMEM_LIMIT),
        cost_estimate=pl.CostEstimate(
            flops=2 * rows * feats * width,
            bytes_accessed=2 * (rows * feats + feats * width + 2 * rows * width),
            transcendentals=0,
        ),
        name="project",
    )(shard_rows, attended, gate, residual, *shards)


CHUNKS = (3, 2, 2)


def on_device_paired(
    query_rows, key_rows, value_rows, key_tiles, tile_counts, out_weight, gate_scale, residual
):
    heads, ntiles, _ = key_tiles.shape
    qkv = (query_rows[0], key_rows[0], value_rows[0])
    query, keys, values = qkv
    rows, feats = query.shape
    hd = feats // heads
    shards = lax.axis_size("dp")
    half = out_weight.shape[1] // 2

    chips = shards // 2
    walk = list(range(0, chips, 2)) + list(range(1, chips, 2))[::-1]
    onward = [
        (2 * walk[p] + c, 2 * walk[(p + 1) % chips] + c) for p in range(chips) for c in range(2)
    ]
    back = [(b, a) for a, b in onward]
    swap = [(i, i ^ 1) for i in range(shards)]
    table = []
    for i in range(shards):
        at = walk.index(i // 2)
        steps = [0] + [d for s in range(1, chips // 2) for d in (-s, s)] + [chips // 2]
        table.append(
            [2 * walk[(at + d) % chips] + c for c in (i % 2, 1 - i % 2) for d in steps]
        )
    dp_index = lax.axis_index("dp")
    shard_rows = lax.dynamic_index_in_dim(jnp.array(table, jnp.int32), dp_index, 0, keepdims=False)

    def send(array, pairs):
        return lax.ppermute(array, "dp", pairs)

    fore, aft = [send(out_weight, onward)], [send(out_weight, back)]
    mine = [out_weight]
    theirs = [send(out_weight, swap)]

    order, bits, crossing = make_plan(key_tiles, tile_counts)
    crossing = crossing[0]
    seq_index = lax.axis_index("seq").astype(jnp.int32)
    near = heads - crossing

    exchange = [(0, 1), (1, 0)]
    far = []
    first = 0
    for many in CHUNKS:
        packed = pack_heads(order, jnp.int32(first), keys, values, many, hd)
        far.append((first, many, lax.ppermute(packed, "seq", exchange)))
        first += many
    sent = first

    def work(start, until, chunk_first, far_rows, attended, likely):
        place = jnp.stack([start, crossing, seq_index, until - start, jnp.int32(chunk_first)])
        return attend_items(order, bits, place, qkv, far_rows, attended, ntiles, hd, likely)

    def work_near(piece, pieces, attended):
        start, until = (near * k // pieces for k in (piece, piece + 1))
        return work(start, until, 0, far_none, attended, 1)

    def work_far(chunk, attended):
        first, many, far_rows = far[chunk]
        start, until = (near + jnp.minimum(crossing, k) for k in (first, first + many))
        return work(start, until, first, far_rows, attended, many)

    def ring_stage(attended):
        attended, f, b = lax.optimization_barrier((attended, fore[-1], aft[-1]))
        mine.extend([f, b])
        fore.append(send(f, onward))
        aft.append(send(b, back))
        theirs.extend([send(f, swap), send(b, swap)])
        return attended

    far_none = unset((1, 2, rows, hd), keys.dtype)
    attended = unset((rows, feats), query.dtype)
    attended = work_near(0, 3, attended)
    attended = ring_stage(attended)
    attended = work_near(1, 3, attended)
    attended = work_near(2, 3, attended)
    attended = ring_stage(attended)
    attended = work_far(0, attended)

    attended, f, b = lax.optimization_barrier((attended, fore[-1], aft[-1]))
    mine.extend([f, b])
    left, right = send(f[:, :half], onward), send(b[:, half:], back)
    theirs.extend([send(f, swap), send(b, swap)])
    attended = work_far(1, attended)
    attended, left, right = lax.optimization_barrier((attended, left, right))
    mine.extend([left, right])
    theirs.extend([send(left, swap), send(right, swap)])
    attended = work_far(2, attended)

    def one_more(i, attended):
        packed = pack_heads(order, i, keys, values, 1, hd)
        far_rows = lax.ppermute(packed, "seq", exchange)
        return work(near + i, near + i + 1, i, far_rows, attended, 1)

    attended = lax.fori_loop(sent, jnp.maximum(crossing, sent), one_more, attended)
    return project(attended, shard_rows, mine + theirs, gate_scale, residual[0])[None]


def solution(mesh):
    in_specs = (
        P("dp", "seq", None),
        P("dp", "seq", None),
        P("dp", "seq", None),
        P(),
        P(),
        P("dp", None),
        P("dp", None),
        P("dp", "seq", None),
    )
    out_specs = P("dp", "seq", None)

    def program(query_rows, key_rows, value_rows, key_tiles, *rest):
        heads = key_tiles.shape[0]
        paired = mesh.shape["seq"] == 2 and mesh.shape["dp"] == heads == 16
        return jax.shard_map(
            on_device_paired if paired else on_device_general,
            mesh=mesh,
            in_specs=in_specs,
            out_specs=out_specs,
            check_vma=False,
        )(query_rows, key_rows, value_rows, key_tiles, *rest)

    return program
```

```python
import functools
import math

import jax
import jax.numpy as jnp
from jax import lax
from jax.experimental import pallas as pl
from jax.experimental.pallas import tpu as pltpu
from jax.sharding import PartitionSpec as P

VMEM_LIMIT = 48 * 1024 * 1024
PROJECT_VMEM = 57 * 1024 * 1024


def slot_scores(query_blocks, key_blocks, value_blocks, head_tiles, slot_index, scale):
    chosen = lax.dynamic_index_in_dim(head_tiles, slot_index, 1, keepdims=False)
    near_keys = jnp.take(key_blocks, chosen, axis=0)
    near_values = jnp.take(value_blocks, chosen, axis=0)
    scores = (
        jnp.einsum("tqd,tkd->tqk", query_blocks, near_keys, preferred_element_type=jnp.float32)
        * scale
    )
    return (scores, near_values)


def attend_head(query_blocks, key_blocks, value_blocks, head_tiles, head_counts, scale):
    scores, near_values = slot_scores(query_blocks, key_blocks, value_blocks, head_tiles, 0, scale)
    row_peak = jnp.max(scores, axis=2)
    weights = jnp.exp(scores - row_peak[:, :, None])
    row_total = jnp.sum(weights, axis=2)
    running = jnp.einsum(
        "tqk,tkd->tqd",
        weights.astype(jnp.bfloat16),
        near_values,
        preferred_element_type=jnp.float32,
    )

    def one_slot(slot_index, carry):
        row_peak, row_total, running = carry
        scores, near_values = slot_scores(
            query_blocks, key_blocks, value_blocks, head_tiles, slot_index, scale
        )
        active = (slot_index < head_counts)[:, None]
        new_peak = jnp.where(active, jnp.maximum(row_peak, jnp.max(scores, axis=2)), row_peak)
        weights = jnp.where(active[:, :, None], jnp.exp(scores - new_peak[:, :, None]), 0.0)
        rescale = jnp.exp(row_peak - new_peak)
        row_total = row_total * rescale + jnp.sum(weights, axis=2)
        running = running * rescale[:, :, None] + jnp.einsum(
            "tqk,tkd->tqd",
            weights.astype(jnp.bfloat16),
            near_values,
            preferred_element_type=jnp.float32,
        )
        return (new_peak, row_total, running)

    last_slot = jnp.max(head_counts)
    row_peak, row_total, running = lax.fori_loop(
        1, last_slot, one_slot, (row_peak, row_total, running)
    )
    return (running / row_total[:, :, None]).astype(jnp.bfloat16)


def head_blocks(rows, first_col, head_dim, ntiles, tile_len):
    return rows[:, first_col : first_col + head_dim].reshape(ntiles, tile_len, head_dim)


def on_device_general(
    query_rows, key_rows, value_rows, key_tiles, tile_counts, out_weight, gate_scale, residual
):
    groups = lax.axis_size("seq")
    seq_index = lax.axis_index("seq")
    tok_rows = query_rows.shape[1]
    feat_width = query_rows.shape[2]
    head_count = key_tiles.shape[0]
    ntiles = key_tiles.shape[1]
    head_dim = feat_width // head_count
    local_heads = head_count // groups
    seqlen = tok_rows * groups
    tile_len = seqlen // ntiles
    scale = 1.0 / math.sqrt(head_dim)
    heads_query, heads_key, heads_value = (
        lax.all_to_all(rows[0], "seq", split_axis=1, concat_axis=0, tiled=True)
        for rows in (query_rows, key_rows, value_rows)
    )
    outputs = []
    for slot_head in range(local_heads):
        global_head = seq_index * local_heads + slot_head
        head_tiles = lax.dynamic_index_in_dim(key_tiles, global_head, 0, keepdims=False)
        head_counts = lax.dynamic_index_in_dim(tile_counts, global_head, 0, keepdims=False)
        first_col = slot_head * head_dim
        mixed_head = attend_head(
            head_blocks(heads_query, first_col, head_dim, ntiles, tile_len),
            head_blocks(heads_key, first_col, head_dim, ntiles, tile_len),
            head_blocks(heads_value, first_col, head_dim, ntiles, tile_len),
            head_tiles,
            head_counts,
            scale,
        )
        outputs.append(mixed_head.reshape(seqlen, head_dim))
    attended = jnp.concatenate(outputs, axis=1)
    token_major = lax.all_to_all(attended, "seq", split_axis=0, concat_axis=1, tiled=True)
    projected = jnp.dot(
        token_major,
        lax.all_gather(out_weight, "dp", axis=0, tiled=True),
        preferred_element_type=jnp.float32,
    )
    block_out = (
        residual[0].astype(jnp.float32) + gate_scale[0].astype(jnp.float32)[None, :] * projected
    )
    return block_out.astype(jnp.bfloat16)[None]


def plan_kernel(heads, ntiles, tiles_ref, counts_ref, order_ref, bits_ref, cross_ref):
    half = ntiles // 2

    def one_head(h, crossing):
        reach = jnp.int32(0)
        for s in range(ntiles):
            count = counts_ref[s, h]
            mask = jnp.int32(0)
            for slot in range(ntiles):
                bit = jnp.left_shift(jnp.int32(1), tiles_ref[s, slot, h])
                mask = mask | jnp.where(slot < count, bit, 0)
            bits_ref[h * ntiles + s] = mask
            other = ((1 << ntiles) - (1 << half)) if s < half else ((1 << half) - 1)
            reach = reach | (mask & other)
        is_cross = (reach != 0).astype(jnp.int32)
        place = jnp.where(is_cross == 1, crossing, heads - 1 - (h - crossing))
        order_ref[place] = h
        return crossing + is_cross

    cross_ref[0] = lax.fori_loop(0, heads, one_head, jnp.int32(0))


def make_plan(key_tiles, tile_counts):
    heads, ntiles, _ = key_tiles.shape
    smem = pl.BlockSpec(memory_space=pltpu.SMEM)
    return pl.pallas_call(
        functools.partial(plan_kernel, heads, ntiles),
        out_shape=(
            jax.ShapeDtypeStruct((heads,), jnp.int32),
            jax.ShapeDtypeStruct((heads * ntiles,), jnp.int32),
            jax.ShapeDtypeStruct((1,), jnp.int32),
        ),
        in_specs=[smem, smem],
        out_specs=(smem, smem, smem),
        name="plan",
    )(key_tiles.transpose(1, 2, 0), tile_counts.transpose(1, 0))


def pack_kernel(many, hd, order_ref, first_ref, key_ref, value_ref, out_ref, held, in_sems, out_sems):
    arriving, leaving = [], []
    for i in range(many):
        col = pl.multiple_of(order_ref[first_ref[0] + i] * hd, hd)
        for j, ref in enumerate((key_ref, value_ref)):
            k = 2 * i + j
            arriving.append(
                pltpu.make_async_copy(ref.at[:, pl.ds(col, hd)], held.at[i, j], in_sems.at[k])
            )
            leaving.append(pltpu.make_async_copy(held.at[i, j], out_ref.at[i, j], out_sems.at[k]))
    for copy in arriving:
        copy.start()
    for copy, onward in zip(arriving, leaving):
        copy.wait()
        onward.start()
    for onward in leaving:
        onward.wait()


def pack_heads(order, first, keys, values, many, hd):
    rows = keys.shape[0]
    smem = pl.BlockSpec(memory_space=pltpu.SMEM)
    anywhere = pl.BlockSpec(memory_space=pl.ANY)
    return pl.pallas_call(
        functools.partial(pack_kernel, many, hd),
        out_shape=jax.ShapeDtypeStruct((many, 2, rows, hd), keys.dtype),
        in_specs=[smem, smem, anywhere, anywhere],
        out_specs=anywhere,
        scratch_shapes=[
            pltpu.VMEM((many, 2, rows, hd), keys.dtype),
            pltpu.SemaphoreType.DMA((2 * many,)),
            pltpu.SemaphoreType.DMA((2 * many,)),
        ],
        compiler_params=pltpu.CompilerParams(vmem_limit_bytes=VMEM_LIMIT),
        cost_estimate=pl.CostEstimate(
            flops=0, bytes_accessed=many * 4 * rows * hd * 2, transcendentals=0
        ),
        name="pack",
    )(order, first.reshape(1), keys, values)


def attend(query, keys, values, exponent_scale, parts):
    rows, hd = query.shape
    scores = [
        lax.dot_general(query, k, (((1,), (1,)), ((), ())), preferred_element_type=jnp.float32)
        for k in keys
    ]
    mixed = []
    for part in range(parts):
        here = slice(part * rows // parts, (part + 1) * rows // parts)
        mine = [s[here, :] for s in scores]
        peak = functools.reduce(jnp.maximum, [jnp.max(s, axis=1, keepdims=True) for s in mine])
        sums = functools.reduce(
            jnp.add,
            [
                jnp.dot(
                    jnp.exp2((s - peak) * exponent_scale).astype(jnp.bfloat16),
                    v,
                    preferred_element_type=jnp.float32,
                )
                for s, v in zip(mine, values)
            ],
        )
        mixed.append((sums[:, :hd] / sums[:, hd:]).astype(jnp.bfloat16))
    return mixed


def attention_kernel(
    work, heads, ntiles, tile_len, scale, order_ref, bits_ref, cross_ref, ids_ref, extra_ref,
    query, keys, values, far, _, out, near_vals, far_vals
):
    half = ntiles // 2
    rows = half * tile_len
    hd = query.shape[1] // heads
    crossing = cross_ref[0]
    seq_index = ids_ref[0]
    near = heads - crossing
    start, until, chunk_first = work(near, crossing, extra_ref[0])
    many = until - start
    near_first = seq_index * half
    far_first = half - near_first
    exponent_scale = scale * math.log2(math.e)

    def item_head(i):
        item = start + i
        return order_ref[jnp.where(item < near, crossing + item, item - near)]

    def column(i):
        return (0, item_head(i))

    def far_block(i):
        return (jnp.maximum(start + i - near - chunk_first, 0), 0, 0, 0)

    def one_item(q_ref, k_ref, v_ref, far_ref, out_ref):
        head = item_head(pl.program_id(0))
        near_vals[:, :hd] = v_ref[...]
        far_vals[:, :hd] = far_ref[0, 1]

        def sees(tile):
            mask = bits_ref[head * ntiles + near_first + tile]
            wide = (lax.shift_right_logical(mask, near_first) & 3) == 3
            reach = (lax.shift_right_logical(mask, far_first) & 3) != 0
            return 2 * wide.astype(jnp.int32) + reach.astype(jnp.int32)

        def run(kind, first, tiles):
            here = pl.ds(first, tiles * tile_len)
            seen = pl.ds(0, rows) if kind & 2 else here
            see_keys, see_values = [k_ref[seen, :]], [near_vals[seen, :]]
            if kind & 1:
                see_keys.append(far_ref[0, 0, seen, :])
                see_values.append(far_vals[seen, :])
            mixed = attend(q_ref[here, :], see_keys, see_values, exponent_scale, tiles)
            for tile in range(tiles):
                out_ref[pl.ds(first + tile * tile_len, tile_len), :] = mixed[tile]

        def all_tiles(kind):
            if kind & 2:
                run(kind, 0, half)
            else:
                for tile in range(half):
                    run(kind, tile * tile_len, 1)

        kinds = [sees(tile) for tile in range(half)]
        same = kinds[0] == kinds[1]
        for kind in range(4):
            pl.when(same & (kinds[0] == kind))(functools.partial(all_tiles, kind))

        @pl.when(jnp.logical_not(same))
        def _():
            def one_tile(tile, _):
                first = pl.multiple_of(tile * tile_len, tile_len)
                for kind in range(4):
                    pl.when(sees(tile) == kind)(functools.partial(run, kind, first, 1))
                return 0

            lax.fori_loop(0, half, one_tile, 0)

    block = pl.BlockSpec((rows, hd), column)
    pipeline = pltpu.emit_pipeline(
        one_item,
        grid=(many,),
        in_specs=[block, block, block, pl.BlockSpec((1, 2, rows, hd), far_block)],
        out_specs=[block],
    )

    @pl.when(many > 0)
    def _():
        ones = jnp.ones((rows, hd), near_vals.dtype)
        near_vals[:, hd:] = ones
        far_vals[:, hd:] = ones
        pipeline(query, keys, values, far, out)


def attend_items(work, plan, ids, extra, qkv, far, attended, ntiles, hd):
    query, keys, values = qkv
    rows, width = query.shape
    heads = width // hd
    tile_len = rows * 2 // ntiles
    smem = pl.BlockSpec(memory_space=pltpu.SMEM)
    anywhere = pl.BlockSpec(memory_space=pl.ANY)
    return pl.pallas_call(
        functools.partial(
            attention_kernel, work, heads, ntiles, tile_len, 1.0 / math.sqrt(hd)
        ),
        out_shape=jax.ShapeDtypeStruct((rows, width), query.dtype),
        in_specs=[smem] * 5 + [anywhere] * 5,
        out_specs=anywhere,
        input_output_aliases={9: 0},
        scratch_shapes=[pltpu.VMEM((rows, 2 * hd), query.dtype)] * 2,
        compiler_params=pltpu.CompilerParams(vmem_limit_bytes=VMEM_LIMIT),
        cost_estimate=pl.CostEstimate(
            flops=rows * rows * hd, bytes_accessed=rows * hd * 2, transcendentals=0
        ),
        name="attend",
    )(*plan, ids, extra, query, keys, values, far, attended)


def empty_kernel(out_ref):
    pass


def unset(shape, dtype):
    return pl.pallas_call(
        empty_kernel,
        out_shape=jax.ShapeDtypeStruct(shape, dtype),
        out_specs=pl.BlockSpec(memory_space=pl.ANY),
        name="unset",
    )()


def project_kernel(depth, rows_ref, ids_ref, att_ref, gate_ref, res_ref, *refs):
    shards, out_ref, weight = refs[:-2], refs[-2], refs[-1]
    dp_index = ids_ref[1]
    core = dp_index & 1
    per_core = len(shards) // 2
    slot = 0

    def put(slot, ref):
        first = pl.multiple_of(rows_ref[dp_index, slot] * depth, depth)
        weight[pl.ds(first, depth), :] = ref[...]

    for owner in range(2):
        mine = shards[owner * per_core : (owner + 1) * per_core]
        for ref in mine[:-2]:
            put(slot, ref)
            slot += 1
        pl.when(core == owner)(functools.partial(put, slot, mine[-2]))
        pl.when(core != owner)(functools.partial(put, slot, mine[-1]))
        slot += 1

    gate = gate_ref[...].astype(jnp.float32)
    projected = jnp.dot(att_ref[...], weight[...], preferred_element_type=jnp.float32)
    out_ref[...] = (res_ref[...].astype(jnp.float32) + gate * projected).astype(out_ref.dtype)


def project(attended, table, ids, shards, gate, residual):
    rows, feats = attended.shape
    width = residual.shape[1]
    depth = shards[0].shape[0]
    block = 512
    here = pl.BlockSpec((rows, block), lambda j, *_: (0, j))
    shard = pl.BlockSpec((depth, block), lambda j, *_: (0, j))
    return pl.pallas_call(
        functools.partial(project_kernel, depth),
        out_shape=jax.ShapeDtypeStruct(residual.shape, residual.dtype),
        grid_spec=pltpu.PrefetchScalarGridSpec(
            num_scalar_prefetch=2,
            grid=(width // block,),
            in_specs=[
                pl.BlockSpec((rows, feats), lambda j, *_: (0, 0)),
                pl.BlockSpec((1, block), lambda j, *_: (0, j)),
                here,
            ]
            + [shard] * len(shards),
            out_specs=here,
            scratch_shapes=[pltpu.VMEM((feats, block), attended.dtype)],
        ),
        compiler_params=pltpu.CompilerParams(vmem_limit_bytes=PROJECT_VMEM),
        cost_estimate=pl.CostEstimate(
            flops=2 * rows * feats * width,
            bytes_accessed=2 * (rows * feats + feats * width + 2 * rows * width),
            transcendentals=0,
        ),
        name="project",
    )(table, ids, attended, gate, residual, *shards)


CHUNKS = (4, 3)


def on_device_paired(
    query_rows, key_rows, value_rows, key_tiles, tile_counts, out_weight, gate_scale, residual
):
    heads, ntiles, _ = key_tiles.shape
    qkv = (query_rows[0], key_rows[0], value_rows[0])
    query, keys, values = qkv
    rows, feats = query.shape
    hd = feats // heads
    shards = lax.axis_size("dp")

    chips = shards // 2
    walk = list(range(0, chips, 2)) + list(range(1, chips, 2))[::-1]
    onward = [
        (2 * walk[p] + c, 2 * walk[(p + 1) % chips] + c) for p in range(chips) for c in range(2)
    ]
    back = [(b, a) for a, b in onward]
    swap = [(i, i ^ 1) for i in range(shards)]
    table = []
    for i in range(shards):
        at = walk.index(i // 2)
        steps = [0] + [d for s in range(1, chips // 2) for d in (-s, s)] + [chips // 2]
        table.append(
            [2 * walk[(at + d) % chips] + c for c in (i % 2, 1 - i % 2) for d in steps]
        )
    table = jnp.array(table, jnp.int32)

    def send(array, pairs):
        return lax.ppermute(array, "dp", pairs)

    fore, aft = [send(out_weight, onward)], [send(out_weight, back)]
    mine = [out_weight]
    theirs = [send(out_weight, swap)]

    plan = make_plan(key_tiles, tile_counts)
    order, _, crossing = plan
    ids = jnp.stack([lax.axis_index("seq"), lax.axis_index("dp")]).astype(jnp.int32)
    zero = jnp.zeros((1,), jnp.int32)

    exchange = [(0, 1), (1, 0)]
    firsts = [sum(CHUNKS[:k]) for k in range(len(CHUNKS))]

    def pack(chunk, order):
        return pack_heads(order, jnp.int32(firsts[chunk]), keys, values, CHUNKS[chunk], hd)

    def swap_frames(packed):
        return lax.ppermute(packed, "seq", exchange)

    def work_near(piece, pieces, attended):
        def work(near, crossing, extra):
            return lax.div(near * piece, pieces), lax.div(near * (piece + 1), pieces), 0

        return attend_items(work, plan, ids, zero, qkv, far_none, attended, ntiles, hd)

    def work_far(chunk, far, attended, skip=0, many=None):
        first = firsts[chunk]
        many = CHUNKS[chunk] if many is None else many

        def work(near, crossing, extra):
            start, until = (
                near + jnp.minimum(crossing, first + k) for k in (skip, skip + many)
            )
            return start, until, first

        return attend_items(work, plan, ids, zero, qkv, far, attended, ntiles, hd)

    def arrive(attended):
        swapped = theirs[-2:]
        attended, f, b, *swapped = lax.optimization_barrier((attended, fore[-1], aft[-1], *swapped))
        theirs[-2:] = swapped
        mine.extend([f, b])
        theirs.extend([send(f, swap), send(b, swap)])
        return attended, f, b

    def ring_stage(attended):
        attended, f, b = arrive(attended)
        fore.append(send(f, onward))
        aft.append(send(b, back))
        return attended

    far_none = unset((1, 2, rows, hd), keys.dtype)
    attended = unset((rows, feats), query.dtype)
    packed0, order1 = lax.optimization_barrier((pack(0, order), order))
    far0 = swap_frames(packed0)
    packed1, attended = lax.optimization_barrier((pack(1, order1), attended))
    far1 = swap_frames(packed1)
    attended = work_near(0, 2, attended)
    attended = ring_stage(attended)
    attended = work_near(1, 2, attended)
    attended = ring_stage(attended)
    attended = work_far(0, far0, attended)

    attended, f, b = arrive(attended)
    way0 = send(f, [pair for pair in onward if pair[0] & 1 == 0])
    way1 = send(b, [pair for pair in back if pair[0] & 1 == 1])
    attended = work_far(1, far1, attended, many=CHUNKS[1] - 1)
    attended, way0, way1, *swapped = lax.optimization_barrier((attended, way0, way1, *theirs[-2:]))
    theirs[-2:] = swapped
    mine.extend([way0, way1])
    theirs.extend(
        [
            send(way0, [pair for pair in swap if pair[0] & 1 == 0]),
            send(way1, [pair for pair in swap if pair[0] & 1 == 1]),
        ]
    )
    attended = work_far(1, far1, attended, skip=CHUNKS[1] - 1, many=1)

    def one_more(i, attended):
        packed = pack_heads(order, i, keys, values, 1, hd)

        def work(near, crossing, extra):
            return near + extra, near + extra + 1, extra

        return attend_items(
            work, plan, ids, i.reshape(1), qkv, swap_frames(packed), attended, ntiles, hd
        )

    sent = sum(CHUNKS)
    attended = lax.fori_loop(sent, jnp.maximum(crossing[0], sent), one_more, attended)
    return project(attended, table, ids, mine + theirs, gate_scale, residual[0])[None]


def solution(mesh):
    in_specs = (
        P("dp", "seq", None),
        P("dp", "seq", None),
        P("dp", "seq", None),
        P(),
        P(),
        P("dp", None),
        P("dp", None),
        P("dp", "seq", None),
    )
    out_specs = P("dp", "seq", None)

    def program(query_rows, key_rows, value_rows, key_tiles, *rest):
        heads = key_tiles.shape[0]
        paired = mesh.shape["seq"] == 2 and mesh.shape["dp"] == heads == 16
        return jax.shard_map(
            on_device_paired if paired else on_device_general,
            mesh=mesh,
            in_specs=in_specs,
            out_specs=out_specs,
            check_vma=False,
        )(query_rows, key_rows, value_rows, key_tiles, *rest)

    return program
```
